256 devices in a mesh: ctx: 16 (over z, x_hi), dec: 8 (over y, x_lo), grp: 2 (over core).
Axes of the slice: x: 4 (x_hi: 2, x_lo: 2; x = x_hi * 2 + x_lo), y: 4, z: 8, core: 2. Of those that a mesh axis runs over, the one named last changes fastest.
Arguments:
- hidden: bfloat16 [3072, 5120], P('ctx', ('dec', 'grp')), may hold values from -6 to 6
- dec_hidden: bfloat16 [4, 64, 5120], P(None, 'ctx', ('dec', 'grp')), may hold values from -6 to 6
- w_down: bfloat16 [5120, 576], P(('dec', 'grp')), may hold values from -0.078125 to 0.078125
- latent_gain: float32 [512], replicated, may hold values from 0.1 to 1.9
- query: bfloat16 [3072, 128, 192], P('ctx', ('dec', 'grp'))
- dec_query: bfloat16 [4, 64, 128, 192], P(None, 'ctx', ('dec', 'grp'))
- w_uk: bfloat16 [128, 128, 512], P(('dec', 'grp')), may hold values from -0.5 to 0.5
- w_uv: bfloat16 [128, 512, 128], P(('dec', 'grp')), may hold values from -0.25 to 0.25
- span_map: int32 [16], replicated, may hold values from 0 to 15, each once
- prompt_len: int32 [64], P('ctx'), may hold values from 1 to 3072, as said below
- block_slot: int32 [48], replicated, may hold values from 0 to 47, each once
Outputs:
- prefill_out: bfloat16 [3072, 128, 128], P('ctx', ('dec', 'grp'))
- decode_out: bfloat16 [4, 64, 128, 128], P(None, 'ctx', ('dec', 'grp'))
- cache: bfloat16 [3072, 576], P('dec')
The draws below stay inside these ranges and needn't reach their ends.
Inputs may be any that keep to these rules, and one draw needn't show every extreme that they name: `span_map`: each span number appears once. Each request's prompt is the first prompt_len tokens of the prompt; some request has all 3072. `block_slot`: each slot appears once.
All inputs are finite; a program needn't handle non-finite values.
Results may differ from the reference program's by a relative error of at most 0.012.
The reference program's roundings to bfloat16 on the way count: a program that leaves them out, or rounds other values in their place, can miss the bound.
Values may be sent and summed in bfloat16 or wider, within the bound.
A program may use at most 128 MiB of HBM per device.

```python
import math
import jax
import jax.numpy as jnp
from jax import lax

D = 5120
H = 128
NOPE = 128
ROPE = 64
LAT = 512
VDIM = 128
SPAN = 192
STEPS = 4
BLK = 64
SEQ = 3072
BATCH = 64
NBLK = 48
N_CTX = 16


def draw_query(key, part):
    key = jax.random.fold_in(key, 11)
    values = jnp.clip(jax.random.normal(key, (SEQ, H, NOPE + ROPE), jnp.float32), -4.0, 4.0)
    return values.astype(jnp.bfloat16)


def draw_dec_query(key, part):
    key = jax.random.fold_in(key, 12)
    values = jnp.clip(jax.random.normal(key, (STEPS, BATCH, H, NOPE + ROPE), jnp.float32), -4.0, 4.0)
    return values.astype(jnp.bfloat16)


def draw_prompt_len(key, part):
    key = jax.random.fold_in(key, 13)
    lengths = jax.random.randint(key, (BATCH,), 1, SEQ + 1, dtype=jnp.int32)
    chosen = jax.random.randint(jax.random.fold_in(key, 1), (), 0, BATCH, dtype=jnp.int32)
    return jnp.where(jnp.arange(BATCH, dtype=jnp.int32) == chosen, SEQ, lengths).astype(jnp.int32)


def level_of(rng, dims, cuts, least, largest):
    loudness, own = 1.0, jax.random.fold_in(rng, 6)
    for dim, parts in cuts:
        heights = jnp.exp(jax.random.uniform(jax.random.fold_in(own, dim), (parts,), jnp.float32, least / len(cuts), largest / len(cuts)))
        loudness = loudness * jnp.repeat(heights, dims[dim] // parts).reshape([-1 if axis == dim else 1 for axis in range(len(dims))])
    return loudness


def centred(own_key, shape, scale, limit, shards=(), held_as=jnp.bfloat16):
    values = jax.random.normal(own_key, shape, jnp.float32) * scale
    if len(shards) > 0:
        values = level_of(own_key, shape, shards, -0.22, 0.18) * values
    return jnp.clip(values, min=-limit, max=limit).astype(held_as)


def setup_inputs(seed: int = 0) -> dict:
    streams_of = jax.random.split(jax.random.key(seed), 12)
    hidden = centred(streams_of[0], (SEQ, D), 1.0, 6.0, ((0, 16), (1, 16)))
    dec_hidden = centred(streams_of[1], (STEPS, BATCH, D), 1.0, 6.0, ((1, 16), (2, 16)))
    w_down = centred(streams_of[2], (D, LAT + ROPE), D ** -0.5, 0.078125, ((0, 16),))
    latent_gain = jnp.clip(1.0 + 0.18 * jax.random.normal(streams_of[3], (LAT,), jnp.float32), 0.1, 1.9)
    query = draw_query(jax.random.fold_in(streams_of[11], 71), 0)
    dec_query = draw_dec_query(jax.random.fold_in(streams_of[11], 71), 0)
    w_uk = centred(streams_of[6], (H, NOPE, LAT), NOPE ** -0.5, 0.5, ((0, 16),))
    w_uv = centred(streams_of[7], (H, LAT, VDIM), LAT ** -0.5, 0.25, ((0, 16),))
    span_map = jax.random.permutation(streams_of[8], N_CTX).astype(jnp.int32)
    prompt_len = draw_prompt_len(jax.random.fold_in(streams_of[11], 71), 0)
    block_slot = jax.random.permutation(streams_of[10], NBLK).astype(jnp.int32)
    return {"hidden": hidden, "dec_hidden": dec_hidden, "w_down": w_down, "latent_gain": latent_gain, "query": query, "dec_query": dec_query, "w_uk": w_uk, "w_uv": w_uv, "span_map": span_map, "prompt_len": prompt_len, "block_slot": block_slot}


EPSILON = 1e-06

def rotate(values, places):
    half = values.shape[-1] // 2
    rates = 10000.0 ** (-jnp.arange(half, dtype=jnp.float32) / half)
    angle = places.astype(jnp.float32)[..., None] * rates
    cosine = jnp.cos(angle)
    sine = jnp.sin(angle)
    first = values[..., :half]
    second = values[..., half:]
    return jnp.concatenate([first * cosine - second * sine, first * sine + second * cosine], axis=-1)

def finish(raw, places, latent_gain):
    latent = raw[..., :LAT]
    normed = latent * lax.rsqrt(lax.optimization_barrier(jnp.mean(latent * latent, axis=-1, keepdims=True)) + EPSILON) * latent_gain
    return jnp.concatenate([normed, rotate(raw[..., LAT:], places)], axis=-1).astype(jnp.bfloat16)

def absorb(query, w_uk, places):
    latent = jnp.einsum('...hk,hkl->...hl', query[..., :NOPE].astype(jnp.float32), w_uk.astype(jnp.float32))
    turned = rotate(query[..., NOPE:].astype(jnp.float32), places[..., None])
    return jnp.concatenate([latent, turned], axis=-1).astype(jnp.bfloat16)

def rounded(weights):
    lowered = weights.astype(jnp.bfloat16)
    return lax.optimization_barrier(lowered).astype(jnp.float32)

def softmax_context(scores, allowed, values):
    masked = jnp.where(allowed, scores, -jnp.inf)
    top = lax.optimization_barrier(jnp.max(masked, axis=-1, keepdims=True))
    weights = jnp.where(allowed, jnp.exp(scores - top), 0.0)
    total = lax.optimization_barrier(jnp.sum(weights, axis=-1, keepdims=True))
    summed = jnp.einsum('...k,kl->...l', rounded(weights), values.astype(jnp.float32))
    return (summed / total).astype(jnp.bfloat16)

def reference(hidden, dec_hidden, w_down, latent_gain, query, dec_query, w_uk, w_uv, span_map, prompt_len, block_slot):
    scale = (NOPE + ROPE) ** (-0.5)
    positions = (span_map[:, None] * SPAN + jnp.arange(SPAN, dtype=jnp.int32)[None, :]).reshape(-1)
    dec_places = prompt_len[None, :] + jnp.arange(STEPS, dtype=jnp.int32)[:, None]
    latent = finish(jnp.dot(hidden, w_down, preferred_element_type=jnp.float32), positions, latent_gain)
    raw_dec = jnp.dot(dec_hidden.reshape(STEPS * BATCH, D), w_down, preferred_element_type=jnp.float32)
    dec_latent = finish(raw_dec.reshape(STEPS, BATCH, LAT + ROPE), dec_places, latent_gain)
    absorbed = absorb(query, w_uk, positions)
    dec_absorbed = absorb(dec_query, w_uk, dec_places)
    group = math.gcd(H, 8)
    keys = latent.astype(jnp.float32)
    causal = positions[None, :] <= positions[:, None]

    def head_block(block):
        block_query, block_uv = block
        scores = jnp.einsum('rhc,sc->hrs', block_query.astype(jnp.float32), keys) * scale
        context = softmax_context(scores, causal[None], latent[:, :LAT])
        return jnp.einsum('hrl,hlv->rhv', context.astype(jnp.float32), block_uv.astype(jnp.float32)).astype(jnp.bfloat16)
    blocks_query = absorbed.reshape(SEQ, H // group, group, LAT + ROPE).transpose(1, 0, 2, 3)
    blocks_uv = w_uv.reshape(H // group, group, LAT, VDIM)
    outputs = lax.map(head_block, (blocks_query, blocks_uv))
    prefill_out = outputs.transpose(1, 0, 2, 3).reshape(SEQ, H, VDIM)
    order = jnp.arange(STEPS, dtype=jnp.int32)
    fresh_ok = order[None, :] <= order[:, None]

    def one_request(item):
        request_query, request_new, length = item
        both = jnp.concatenate([latent, request_new], axis=0)
        allowed = jnp.concatenate([jnp.broadcast_to((positions < length)[None, :], (STEPS, SEQ)), fresh_ok], axis=1)
        scores = jnp.einsum('thc,sc->ths', request_query.astype(jnp.float32), both.astype(jnp.float32)) * scale
        return softmax_context(scores, allowed[:, None, :], both[:, :LAT])
    contexts = lax.map(one_request, (dec_absorbed.transpose(1, 0, 2, 3), dec_latent.transpose(1, 0, 2), prompt_len))
    decode_out = jnp.einsum('bthl,hlv->tbhv', contexts.astype(jnp.float32), w_uv.astype(jnp.float32)).astype(jnp.bfloat16)
    inverse = jnp.zeros((N_CTX,), jnp.int32).at[span_map].set(jnp.arange(N_CTX, dtype=jnp.int32))
    by_place = latent.reshape(N_CTX, SPAN, LAT + ROPE)[inverse].reshape(NBLK, BLK, LAT + ROPE)
    cache = jnp.zeros_like(by_place).at[block_slot].set(by_place).reshape(SEQ, LAT + ROPE)
    return (prefill_out, decode_out, cache)
```

```python
import math

import jax
import jax.numpy as jnp
import numpy as np
from jax import lax
from jax.experimental import pallas as pl
from jax.experimental.pallas import tpu as pltpu
from jax.sharding import PartitionSpec as P

F32 = jnp.float32
BF16 = jnp.bfloat16
MESH = pl.DeviceIdType.MESH

EPSILON = 1e-06
SPAN = 192
HEADS = 8
STEPS = 4
REQS = 4
NOPE = 128
ROPE = 64
LAT = 512
WIDTH = LAT + ROPE
VDIM = 128
PIECE = 16
ROWS = SPAN + STEPS * REQS
CHUNK = 768
BLK = 64
SCALE2 = (NOPE + ROPE) ** -0.5 * math.log2(math.e)
MASKED = -2e30
LOWEST = -1e30


def iota(shape, dim):
    return lax.broadcasted_iota(jnp.int32, shape, dim)


def nt(a, b):
    return lax.dot_general(a, b, (((1,), (1,)), ((), ())), preferred_element_type=F32)


def swapped(v):
    half = v.shape[-1] // 2
    return jnp.concatenate([v[:, half:], v[:, :half]], axis=1)


def tables(places, rates):
    angle = places.astype(F32) * rates
    sign = jnp.where(iota((1, ROPE), 1) < ROPE // 2, -1.0, 1.0)
    return jnp.cos(angle), jnp.sin(angle) * sign


def dec_rows_value(prompt_len, row):
    request = row & (REQS - 1)
    value = jnp.zeros_like(row)
    for b in range(REQS):
        value = jnp.where(request == b, prompt_len[b], value)
    return value


def kernel(
    hidden_h,
    dec_hidden,
    w_down_h,
    gain,
    query_h,
    dec_query,
    w_uk_h,
    w_uv_h,
    rates,
    span_map,
    prompt_len,
    block_slot,
    out,
    dec_out,
    cache,
    hidden,
    w_down,
    query,
    w_uk,
    w_uv,
    dec_f,
    part,
    from_core,
    sums,
    arrived,
    keys,
    dec_lat,
    q_f,
    dq_f,
    q_all,
    acc,
    best,
    total,
    o_f,
    do_f,
    load_sem,
    core_sem,
    rs_send,
    rs_recv,
    z_send,
    z_recv,
    d_recv,
    one_send,
    one_recv,
    two_send,
    two_recv,
    fwd_send,
    fwd_recv,
    x_send,
    x_recv,
):
    ctx = lax.axis_index("ctx")
    dec = lax.axis_index("dec")
    core = lax.axis_index("grp")
    z, x_hi = ctx // 2, ctx % 2
    y, x_lo = dec // 2, dec % 2
    x = x_hi * 2 + x_lo
    other = 1 - core

    def at(x_, y_, z_, c_):
        return (z_ * 2 + x_ // 2, y_ * 2 + x_ % 2, c_)

    def remote(src, dst, send, recv, device):
        return pltpu.make_async_remote_copy(
            src_ref=src,
            dst_ref=dst,
            send_sem=send,
            recv_sem=recv,
            device_id=device,
            device_id_type=MESH,
        )

    me = (ctx, dec, core)
    other_core = (ctx, dec, other)
    x_step = lambda j: at((x + j) % 4, y, z, core)
    y_step = lambda j: at(x, (y + j) % 4, z, core)
    z_step = lambda j: (((z + j) % 8) * 2 + x_hi, dec, core)
    d_step = lambda j: (ctx, (dec + j) % 8, core)
    along = (x_step, y_step)

    loads = [
        pltpu.make_async_copy(src, dst, load_sem.at[i])
        for i, (src, dst) in enumerate(
            ((hidden_h, hidden), (w_down_h, w_down), (query_h, query), (w_uk_h, w_uk), (w_uv_h, w_uv))
        )
    ]
    for load in loads:
        load.start()

    barrier = pltpu.get_barrier_semaphore()
    greeted = [other_core]
    greeted += [d_step(j) for j in range(1, 8)]
    greeted += [z_step(j) for j in range(1, 8)]
    greeted += [(z * 2 + 1 - x_hi, y * 2 + lo, core) for lo in range(2)]
    for device in greeted:
        pl.semaphore_signal(barrier, inc=1, device_id=device, device_id_type=MESH)

    for t in range(STEPS):
        dec_f[t * REQS : (t + 1) * REQS, :] = dec_hidden[t].astype(F32)
    loads[0].wait()
    loads[1].wait()
    weights = w_down[...]
    partial = jnp.dot(hidden[...], weights, preferred_element_type=F32)
    for piece in range(12):
        part[piece % 2, piece // 2] = partial[piece * PIECE : (piece + 1) * PIECE]
    partial = jnp.dot(dec_f[...].astype(BF16), weights, preferred_element_type=F32)
    part[0, 6] = partial
    part[1, 6] = partial

    pl.semaphore_wait(barrier, len(greeted))

    swap = remote(part.at[other], from_core, core_sem.at[0], core_sem.at[1], other_core)
    swap.start()

    row = iota((ROWS, 1), 0)
    my_start = span_map[ctx] * SPAN
    lengths = dec_rows_value(prompt_len, row)
    is_dec = row >= SPAN
    places = jnp.where(is_dec, lengths + ((row - SPAN) >> 2), my_start + row)
    q_limit = jnp.where(is_dec, lengths - 1, my_start + row)
    cosine, sine = tables(places, rates[...])

    loads[2].wait()
    loads[3].wait()
    wide = query[...].astype(F32).reshape(SPAN * HEADS, NOPE + ROPE)
    q_f[0] = wide[:, :NOPE]
    q_f[1, :, :ROPE] = wide[:, NOPE:]
    wide = dec_query[...].astype(F32).reshape(STEPS * REQS * HEADS, NOPE + ROPE)
    dq_f[0] = wide[:, :NOPE]
    dq_f[1, :, :ROPE] = wide[:, NOPE:]

    def absorb(h):
        def both(i):
            mine = q_f[i, pl.ds(h, SPAN, stride=HEADS), :]
            decs = dq_f[i, pl.ds(h, STEPS * REQS, stride=HEADS), :]
            return jnp.concatenate([mine, decs], axis=0)

        nope = both(0).astype(BF16)
        q_all[h, :, :LAT] = jnp.dot(nope, w_uk[h], preferred_element_type=F32).astype(BF16)
        rope = both(1)[:, :ROPE]
        q_all[h, :, LAT:] = (rope * cosine + swapped(rope) * sine).astype(BF16)

    for h in range(4):
        absorb(h)

    swap.wait()
    for s in range(7):
        sums[s] = part[core, s] + from_core[s]

    def rs_copy(j):
        slot = (dec + j + z) % 8
        return slot, remote(
            sums.at[jnp.minimum(slot, 6)], arrived.at[j], rs_send.at[j], rs_recv.at[j], d_step(j)
        )

    for j in range(1, 8):
        slot, copy = rs_copy(j)

        @pl.when(slot != 7)
        def _():
            copy.start()

    for h in range(4, HEADS):
        absorb(h)

    own = (dec + z) % 8
    safe = jnp.minimum(own, 5)
    home = keys.at[0, safe // 3, core, safe % 3]

    @pl.when(own != 7)
    def _():
        raw = sums[jnp.minimum(own, 6)]
        for j in range(1, 8):
            rs_copy(j)[1].wait_recv()
            raw = raw + arrived[j]
        i = iota((PIECE, 1), 0)
        prompt_places = my_start + (2 * own + core) * PIECE + i
        dec_places = dec_rows_value(prompt_len, i) + (i >> 2)
        spots = jnp.where(own == 6, dec_places, prompt_places)
        cos_k, sin_k = tables(spots, rates[...])
        lat = raw[:, :LAT]
        square = jnp.mean(lat * lat, axis=1, keepdims=True)
        lat = lat * lax.rsqrt(square + EPSILON) * gain[...]
        rope = raw[:, LAT:]
        rope = rope * cos_k + swapped(rope) * sin_k
        done = jnp.concatenate([lat, rope], axis=1).astype(BF16)

        @pl.when(own < 6)
        def _():
            keys[0, safe // 3, core, safe % 3] = done

        @pl.when(own == 6)
        def _():
            dec_lat[...] = done

    def z_copy(j):
        return remote(home, home, z_send.at[j], z_recv.at[safe], z_step(j))

    def d_copy(j):
        return remote(dec_lat, dec_lat, z_send.at[j], d_recv.at[0], d_step(j))

    @pl.when(own < 6)
    def _():
        for j in range(1, 8):
            z_copy(j).start()

    @pl.when(own == 6)
    def _():
        for j in range(1, 8):
            d_copy(j).start()

    for s in range(6):

        @pl.when(own != s)
        def _():
            spot = keys.at[0, s // 3, core, s % 3]
            remote(spot, spot, z_send.at[0], z_recv.at[s], me).wait_recv()

    def one_copy(r, j):
        return remote(
            keys.at[0, r, core, pl.ds(0, 3)],
            keys.at[0, r, core, pl.ds(3 * (4 - j), 3)],
            one_send.at[r, j],
            one_recv.at[r, 4 - j],
            along[r](j),
        )

    for j in (1, 3, 2):
        for r in range(2):
            one_copy(r, j).start()

    @pl.when(own != 6)
    def _():
        d_copy(1).wait_recv()

    best[...] = jnp.full(best.shape, LOWEST, F32)
    total[...] = jnp.zeros(total.shape, F32)
    acc[...] = jnp.zeros(acc.shape, F32)
    fresh_keys = dec_lat[...]
    count = HEADS * STEPS * REQS
    fresh = nt(q_all[:, SPAN:, :].reshape(count, WIDTH), fresh_keys) * SCALE2
    r_, c_ = iota((count, PIECE), 0), iota((count, PIECE), 1)
    fresh_ok = jnp.logical_and((r_ & 3) == (c_ & 3), (c_ >> 2) <= ((r_ & 15) >> 2))
    fresh = jnp.where(fresh_ok, fresh, MASKED)
    top = jnp.max(fresh, axis=1, keepdims=True)
    weight = jnp.exp2(fresh - top)
    best[:, SPAN:, :] = top.reshape(HEADS, 16, 1)
    total[:, SPAN:, :] = jnp.sum(weight, axis=1, keepdims=True).reshape(HEADS, 16, 1)
    acc[:, SPAN:, :] = jnp.dot(
        weight.astype(BF16), fresh_keys[:, :LAT], preferred_element_type=F32
    ).reshape(HEADS, 16, LAT)

    for j in (1, 3, 2):
        for r in range(2):
            one_copy(r, j).wait_recv()

    def two_copy(r, k):
        return remote(
            keys.at[0, r, core], keys.at[k, r, core], two_send.at[r, k], two_recv.at[r, k], along[1 - r](4 - k)
        )

    def fwd_copy(r, k):
        half = pl.ds(0, 6) if k == 1 else pl.ds(6, 6)
        return remote(
            keys.at[k, r, core, half],
            keys.at[2, r, core, half],
            fwd_send.at[r, k],
            fwd_recv.at[r, k],
            along[1 - r](4 - k),
        )

    def x_copy(r, k):
        block = keys.at[k, r, core]
        return remote(block, block, x_send.at[r, k], x_recv.at[r, k], other_core)

    def x_wait(k):
        for r in range(2):
            block = keys.at[k, r, other]
            remote(block, block, x_send.at[r, k], x_recv.at[r, k], other_core).wait_recv()

    for k in (1, 3):
        for r in range(2):
            two_copy(r, k).start()
    for r in range(2):
        x_copy(r, 0).start()

    def key_places(k):
        lane = iota((1, CHUNK), 1)
        piece = lane >> 4
        route = jnp.where(piece >= 24, 1, 0)
        rest = piece - 24 * route
        parity = jnp.where(rest >= 12, 1, 0)
        rest = rest - 12 * parity
        dist = (rest * 11) >> 5
        slot = rest - 3 * dist + 3 * route
        x_src = (x + jnp.where(route == 0, dist, k)) & 3
        y_src = (y + jnp.where(route == 0, k, dist)) & 3
        z_src = (slot - (y_src * 2 + (x_src & 1))) & 7
        ctx_src = z_src * 2 + (x_src >> 1)
        span = jnp.zeros_like(lane)
        for i in range(16):
            span = jnp.where(ctx_src == i, span_map[i], span)
        return span * SPAN + (2 * slot + parity) * PIECE + (lane & 15)

    def attend(k):
        ks = keys.at[k]
        allowed = key_places(k) <= q_limit
        allowed = jnp.concatenate([allowed, allowed], axis=0)

        def scores(g):
            return nt(
                q_all[2 * g : 2 * g + 2].reshape(2 * ROWS, WIDTH), ks[...].reshape(CHUNK, WIDTH)
            )

        s = scores(0)
        for g in range(4):
            s_next = scores(g + 1) if g < 3 else None
            hs = slice(2 * g, 2 * g + 2)
            s = jnp.where(allowed, s * SCALE2, MASKED)
            old = best[hs].reshape(2 * ROWS, 1)
            new = jnp.maximum(old, jnp.max(s, axis=1, keepdims=True))
            w = jnp.exp2(s - new)
            factor = jnp.exp2(old - new)
            best[hs] = new.reshape(2, ROWS, 1)
            total[hs] = total[hs] * factor.reshape(2, ROWS, 1) + jnp.sum(
                w, axis=1, keepdims=True
            ).reshape(2, ROWS, 1)
            summed = jnp.dot(
                w.astype(BF16), ks[..., :LAT].reshape(CHUNK, LAT), preferred_element_type=F32
            )
            acc[hs] = acc[hs] * factor.reshape(2, ROWS, 1) + summed.reshape(2, ROWS, LAT)
            s = s_next

    x_wait(0)
    attend(0)
    for k in (1, 3):
        for r in range(2):
            two_copy(r, k).wait_recv()
            fwd_copy(r, k).start()
            x_copy(r, k).start()
    x_wait(1)
    attend(1)
    for r in range(2):
        for k in (1, 3):
            fwd_copy(r, k).wait_recv()
        x_copy(r, 2).start()
    x_wait(3)
    attend(3)
    x_wait(2)
    attend(2)

    loads[4].wait()
    for h in range(HEADS):
        context = (acc[h] / total[h]).astype(BF16)
        value = jnp.dot(context, w_uv[h], preferred_element_type=F32)
        o_f[pl.ds(h, SPAN, stride=HEADS), :] = value[:SPAN]
        do_f[pl.ds(h, STEPS * REQS, stride=HEADS), :] = value[SPAN:]
    out[...] = o_f[...].reshape(SPAN, HEADS, VDIM).astype(BF16)
    dec_out[...] = do_f[...].reshape(STEPS, REQS, HEADS, VDIM).astype(BF16)

    blocks = [jnp.int32(0)] * 6
    for b in range(48):
        slot = block_slot[b]
        for i in range(6):
            blocks[i] = jnp.where(slot == dec * 6 + i, b, blocks[i])
    for i in range(6):
        span = blocks[i] // 3
        c_src = jnp.int32(0)
        for c in range(16):
            c_src = jnp.where(span_map[c] == span, c, c_src)
        z_src, hi_src = c_src >> 1, c_src & 1
        for n in range(4):
            piece = (blocks[i] - span * 3) * 4 + n
            parity, slot = piece & 1, piece >> 1
            d_src = (slot - z_src) & 7
            dy = ((d_src >> 1) - y) & 3
            dx = (hi_src * 2 + (d_src & 1) - x) & 3
            first = slot < 3
            k = jnp.where(first, dy, dx)
            spot = jnp.where(first, dx, dy) * 3 + slot - jnp.where(first, 0, 3)
            cache[i * BLK + n * PIECE : i * BLK + (n + 1) * PIECE, :] = keys[
                k, jnp.where(first, 0, 1), parity, spot
            ]

    for j in range(1, 8):
        slot, copy = rs_copy(j)

        @pl.when(slot != 7)
        def _():
            copy.wait_send()

    @pl.when(own < 6)
    def _():
        for j in range(1, 8):
            z_copy(j).wait_send()

    @pl.when(own == 6)
    def _():
        for j in range(1, 8):
            d_copy(j).wait_send()

    for r in range(2):
        for j in range(1, 4):
            one_copy(r, j).wait_send()
        for k in (1, 3):
            two_copy(r, k).wait_send()
            fwd_copy(r, k).wait_send()
        for k in range(4):
            x_copy(r, k).wait_send()


def shards(
    hidden,
    dec_hidden,
    w_down,
    latent_gain,
    query,
    dec_query,
    w_uk,
    w_uv,
    span_map,
    prompt_len,
    block_slot,
):
    rates = (10000.0 ** (-np.arange(ROPE // 2, dtype=np.float32) / np.float32(ROPE // 2))).astype(
        np.float32
    )
    rates = jnp.asarray(np.concatenate([rates, rates])[None, :])
    hbm = pl.BlockSpec(memory_space=pl.ANY)
    vmem = pl.BlockSpec(memory_space=pltpu.VMEM)
    smem = pl.BlockSpec(memory_space=pltpu.SMEM)
    dma = pltpu.SemaphoreType.DMA
    return pl.pallas_call(
        kernel,
        out_shape=(
            jax.ShapeDtypeStruct((SPAN, HEADS, VDIM), BF16),
            jax.ShapeDtypeStruct((STEPS, REQS, HEADS, VDIM), BF16),
            jax.ShapeDtypeStruct((384, WIDTH), BF16),
        ),
        in_specs=[hbm, vmem, hbm, vmem, hbm, vmem, hbm, hbm, vmem, smem, smem, smem],
        out_specs=(vmem, vmem, vmem),
        scratch_shapes=[
            pltpu.VMEM((SPAN, 320), BF16),
            pltpu.VMEM((320, WIDTH), BF16),
            pltpu.VMEM((SPAN, HEADS, NOPE + ROPE), BF16),
            pltpu.VMEM((HEADS, NOPE, LAT), BF16),
            pltpu.VMEM((HEADS, LAT, VDIM), BF16),
            pltpu.VMEM((STEPS * REQS, 320), F32),
            pltpu.VMEM((2, 7, PIECE, WIDTH), F32),
            pltpu.VMEM((7, PIECE, WIDTH), F32),
            pltpu.VMEM((7, PIECE, WIDTH), F32),
            pltpu.VMEM((8, PIECE, WIDTH), F32),
            pltpu.VMEM((4, 2, 2, 12, PIECE, WIDTH), BF16),
            pltpu.VMEM((PIECE, WIDTH), BF16),
            pltpu.VMEM((2, SPAN * HEADS, NOPE), F32),
            pltpu.VMEM((2, STEPS * REQS * HEADS, NOPE), F32),
            pltpu.VMEM((HEADS, ROWS, WIDTH), BF16),
            pltpu.VMEM((HEADS, ROWS, LAT), F32),
            pltpu.VMEM((HEADS, ROWS, 1), F32),
            pltpu.VMEM((HEADS, ROWS, 1), F32),
            pltpu.VMEM((SPAN * HEADS, VDIM), F32),
            pltpu.VMEM((STEPS * REQS * HEADS, VDIM), F32),
            dma((5,)),
            dma((2,)),
            dma((8,)),
            dma((8,)),
            dma((8,)),
            dma((8,)),
            dma((1,)),
            dma((2, 4)),
            dma((2, 4)),
            dma((2, 4)),
            dma((2, 4)),
            dma((2, 4)),
            dma((2, 4)),
            dma((2, 4)),
            dma((2, 4)),
        ],
        compiler_params=pltpu.CompilerParams(
            collective_id=0, has_side_effects=True, vmem_limit_bytes=56 * 2**20
        ),
    )(
        hidden,
        dec_hidden,
        w_down,
        latent_gain.reshape(1, LAT),
        query,
        dec_query,
        w_uk,
        w_uv,
        rates,
        span_map,
        prompt_len,
        block_slot,
    )


def solution(mesh):
    in_specs = (
        P("ctx", ("dec", "grp")),
        P(None, "ctx", ("dec", "grp")),
        P(("dec", "grp"), None),
        P(),
        P("ctx", ("dec", "grp"), None),
        P(None, "ctx", ("dec", "grp"), None),
        P(("dec", "grp"), None, None),
        P(("dec", "grp"), None, None),
        P(),
        P("ctx"),
        P(),
    )
    out_specs = (
        P("ctx", ("dec", "grp"), None),
        P(None, "ctx", ("dec", "grp"), None),
        P("dec", None),
    )
    return jax.shard_map(shards, mesh=mesh, in_specs=in_specs, out_specs=out_specs, check_vma=False)
```

```python
import math

import jax
import jax.numpy as jnp
import numpy as np
from jax import lax
from jax.experimental import pallas as pl
from jax.experimental.pallas import tpu as pltpu
from jax.sharding import PartitionSpec as P

F32 = jnp.float32
BF16 = jnp.bfloat16
MESH = pl.DeviceIdType.MESH

EPSILON = 1e-06
SPAN = 192
HEADS = 8
STEPS = 4
REQS = 4
NOPE = 128
ROPE = 64
LAT = 512
WIDTH = LAT + ROPE
VDIM = 128
PIECE = 16
ROWS = SPAN + STEPS * REQS
CHUNK = 768
BLK = 64
SCALE2 = (NOPE + ROPE) ** -0.5 * math.log2(math.e)
MASKED = -2e30
LOWEST = -1e30


def iota(shape, dim):
    return lax.broadcasted_iota(jnp.int32, shape, dim)


def nt(a, b):
    return lax.dot_general(a, b, (((1,), (1,)), ((), ())), preferred_element_type=F32)


def swapped(v):
    half = v.shape[-1] // 2
    return jnp.concatenate([v[:, half:], v[:, :half]], axis=1)


def tables(places, rates):
    angle = places.astype(F32) * rates
    sign = jnp.where(iota((1, ROPE), 1) < ROPE // 2, -1.0, 1.0)
    return jnp.cos(angle), jnp.sin(angle) * sign


def dec_rows_value(prompt_len, row):
    request = row & (REQS - 1)
    value = jnp.zeros_like(row)
    for b in range(REQS):
        value = jnp.where(request == b, prompt_len[b], value)
    return value


def kernel(
    hidden_h,
    dec_hidden,
    w_down_h,
    gain,
    query_h,
    dec_query,
    w_uk_h,
    w_uv_h,
    rates,
    span_map,
    prompt_len,
    block_slot,
    out,
    dec_out,
    cache,
    hidden,
    w_down,
    query,
    w_uk,
    w_uv,
    dec_f,
    part,
    from_core,
    sums,
    arrived,
    keys,
    dec_lat,
    q_f,
    dq_f,
    q_all,
    acc,
    best,
    total,
    o_f,
    do_f,
    load_sem,
    core_sem,
    rs_send,
    rs_recv,
    z_send,
    z_recv,
    d_recv,
    one_send,
    one_recv,
    two_send,
    two_recv,
    fwd_send,
    fwd_recv,
    x_send,
    x_recv,
):
    ctx = lax.axis_index("ctx")
    dec = lax.axis_index("dec")
    core = lax.axis_index("grp")
    z, x_hi = ctx // 2, ctx % 2
    y, x_lo = dec // 2, dec % 2
    x = x_hi * 2 + x_lo
    other = 1 - core

    def at(x_, y_, z_, c_):
        return (z_ * 2 + x_ // 2, y_ * 2 + x_ % 2, c_)

    def remote(src, dst, send, recv, device):
        return pltpu.make_async_remote_copy(
            src_ref=src,
            dst_ref=dst,
            send_sem=send,
            recv_sem=recv,
            device_id=device,
            device_id_type=MESH,
        )

    me = (ctx, dec, core)
    other_core = (ctx, dec, other)
    x_step = lambda j: at((x + j) % 4, y, z, core)
    y_step = lambda j: at(x, (y + j) % 4, z, core)
    z_step = lambda j: (((z + j) % 8) * 2 + x_hi, dec, core)
    d_step = lambda j: (ctx, (dec + j) % 8, core)
    along = (x_step, y_step)

    loads = [
        pltpu.make_async_copy(src, dst, load_sem.at[i])
        for i, (src, dst) in enumerate(
            ((hidden_h, hidden), (w_down_h, w_down), (query_h, query), (w_uk_h, w_uk), (w_uv_h, w_uv))
        )
    ]
    for load in loads:
        load.start()

    barrier = pltpu.get_barrier_semaphore()
    greeted = [other_core]
    greeted += [d_step(j) for j in range(1, 8)]
    greeted += [z_step(j) for j in range(1, 8)]
    greeted += [(z * 2 + 1 - x_hi, y * 2 + lo, core) for lo in range(2)]
    for device in greeted:
        pl.semaphore_signal(barrier, inc=1, device_id=device, device_id_type=MESH)

    for t in range(STEPS):
        dec_f[t * REQS : (t + 1) * REQS, :] = dec_hidden[t].astype(F32)
    loads[0].wait()
    loads[1].wait()
    weights = w_down[...]
    partial = jnp.dot(hidden[...], weights, preferred_element_type=F32)
    for piece in range(12):
        part[piece % 2, piece // 2] = partial[piece * PIECE : (piece + 1) * PIECE]
    partial = jnp.dot(dec_f[...].astype(BF16), weights, preferred_element_type=F32)
    part[0, 6] = partial
    part[1, 6] = partial

    blocks = [jnp.int32(0)] * 6
    cache_spots = []
    for b in range(48):
        slot = block_slot[b]
        for i in range(6):
            blocks[i] = jnp.where(slot == dec * 6 + i, b, blocks[i])
    for i in range(6):
        span = blocks[i] // 3
        c_src = jnp.int32(0)
        for c in range(16):
            c_src = jnp.where(span_map[c] == span, c, c_src)
        z_from, hi_from = c_src >> 1, c_src & 1
        for n in range(4):
            piece = (blocks[i] - span * 3) * 4 + n
            parity, slot = piece & 1, piece >> 1
            d_from = (slot - z_from) & 7
            dy = ((d_from >> 1) - y) & 3
            dx = (hi_from * 2 + (d_from & 1) - x) & 3
            first = slot < 3
            k = jnp.where(first, dy, dx)
            spot = jnp.where(first, dx, dy) * 3 + slot - jnp.where(first, 0, 3)
            cache_spots.append((k, jnp.where(first, 0, 1), parity, spot))

    pl.semaphore_wait(barrier, len(greeted))

    swap = remote(part.at[other], from_core, core_sem.at[0], core_sem.at[1], other_core)
    swap.start()

    row = iota((ROWS, 1), 0)
    my_start = span_map[ctx] * SPAN
    lengths = dec_rows_value(prompt_len, row)
    is_dec = row >= SPAN
    places = jnp.where(is_dec, lengths + ((row - SPAN) >> 2), my_start + row)
    q_limit = jnp.where(is_dec, lengths - 1, my_start + row)
    cosine, sine = tables(places, rates[...])
    q_limit = jnp.concatenate([q_limit, q_limit], axis=0)

    loads[2].wait()
    loads[3].wait()
    wide = query[...].astype(F32).reshape(SPAN * HEADS, NOPE + ROPE)
    q_f[0] = wide[:, :NOPE]
    q_f[1, :, :ROPE] = wide[:, NOPE:]
    wide = dec_query[...].astype(F32).reshape(STEPS * REQS * HEADS, NOPE + ROPE)
    dq_f[0] = wide[:, :NOPE]
    dq_f[1, :, :ROPE] = wide[:, NOPE:]

    def absorb(h):
        def both(i):
            mine = q_f[i, pl.ds(h, SPAN, stride=HEADS), :]
            decs = dq_f[i, pl.ds(h, STEPS * REQS, stride=HEADS), :]
            return jnp.concatenate([mine, decs], axis=0)

        nope = both(0).astype(BF16)
        q_all[h, :, :LAT] = jnp.dot(nope, w_uk[h], preferred_element_type=F32).astype(BF16)
        rope = both(1)[:, :ROPE]
        q_all[h, :, LAT:] = (rope * cosine + swapped(rope) * sine).astype(BF16)

    for h in range(4):
        absorb(h)

    swap.wait()
    for s in range(7):
        sums[s] = part[core, s] + from_core[s]

    def rs_copy(j):
        slot = (dec + j + z) % 8
        return slot, remote(
            sums.at[jnp.minimum(slot, 6)], arrived.at[j], rs_send.at[j], rs_recv.at[j], d_step(j)
        )

    for j in range(1, 8):
        slot, copy = rs_copy(j)

        @pl.when(slot != 7)
        def _():
            copy.start()

    for h in range(4, HEADS):
        absorb(h)

    own = (dec + z) % 8
    safe = jnp.minimum(own, 5)
    home = keys.at[0, safe // 3, core, safe % 3]

    @pl.when(own != 7)
    def _():
        raw = sums[jnp.minimum(own, 6)]
        for j in range(1, 8):
            rs_copy(j)[1].wait_recv()
            raw = raw + arrived[j]
        i = iota((PIECE, 1), 0)
        prompt_places = my_start + (2 * own + core) * PIECE + i
        dec_places = dec_rows_value(prompt_len, i) + (i >> 2)
        spots = jnp.where(own == 6, dec_places, prompt_places)
        cos_k, sin_k = tables(spots, rates[...])
        lat = raw[:, :LAT]
        square = jnp.mean(lat * lat, axis=1, keepdims=True)
        lat = lat * lax.rsqrt(square + EPSILON) * gain[...]
        rope = raw[:, LAT:]
        rope = rope * cos_k + swapped(rope) * sin_k
        done = jnp.concatenate([lat, rope], axis=1).astype(BF16)

        @pl.when(own < 6)
        def _():
            keys[0, safe // 3, core, safe % 3] = done

        @pl.when(own == 6)
        def _():
            dec_lat[...] = done

    def z_copy(j):
        return remote(home, home, z_send.at[j], z_recv.at[safe], z_step(j))

    def d_copy(j):
        return remote(dec_lat, dec_lat, z_send.at[j], d_recv.at[0], d_step(j))

    @pl.when(own < 6)
    def _():
        for j in range(1, 8):
            z_copy(j).start()

    @pl.when(own == 6)
    def _():
        for j in range(1, 8):
            d_copy(j).start()

    for s in range(6):

        @pl.when(own != s)
        def _():
            spot = keys.at[0, s // 3, core, s % 3]
            remote(spot, spot, z_send.at[0], z_recv.at[s], me).wait_recv()

    def one_copy(r, j):
        return remote(
            keys.at[0, r, core, pl.ds(0, 3)],
            keys.at[0, r, core, pl.ds(3 * (4 - j), 3)],
            one_send.at[r, j],
            one_recv.at[r, 4 - j],
            along[r](j),
        )

    for j in (1, 3, 2):
        for r in range(2):
            one_copy(r, j).start()

    @pl.when(own != 6)
    def _():
        d_copy(1).wait_recv()

    best[...] = jnp.full(best.shape, LOWEST, F32)
    total[...] = jnp.zeros(total.shape, F32)
    acc[...] = jnp.zeros(acc.shape, F32)
    fresh_keys = dec_lat[...]
    count = HEADS * STEPS * REQS
    fresh = nt(q_all[:, SPAN:, :].reshape(count, WIDTH), fresh_keys) * SCALE2
    r_, c_ = iota((count, PIECE), 0), iota((count, PIECE), 1)
    fresh_ok = jnp.logical_and((r_ & 3) == (c_ & 3), (c_ >> 2) <= ((r_ & 15) >> 2))
    fresh = jnp.where(fresh_ok, fresh, MASKED)
    top = jnp.max(fresh, axis=1, keepdims=True)
    weight = jnp.exp2(fresh - top)
    best[:, SPAN:, :] = top.reshape(HEADS, 16, 1)
    total[:, SPAN:, :] = jnp.sum(weight, axis=1, keepdims=True).reshape(HEADS, 16, 1)
    acc[:, SPAN:, :] = jnp.dot(
        weight.astype(BF16), fresh_keys[:, :LAT], preferred_element_type=F32
    ).reshape(HEADS, 16, LAT)

    for j in (1, 3, 2):
        for r in range(2):
            one_copy(r, j).wait_recv()

    def two_copy(r, k):
        return remote(
            keys.at[0, r, core], keys.at[k, r, core], two_send.at[r, k], two_recv.at[r, k], along[1 - r](4 - k)
        )

    def fwd_copy(r, k):
        half = pl.ds(0, 6) if k == 1 else pl.ds(6, 6)
        return remote(
            keys.at[k, r, core, half],
            keys.at[2, r, core, half],
            fwd_send.at[r, k],
            fwd_recv.at[r, k],
            along[1 - r](4 - k),
        )

    def x_copy(r, k):
        block = keys.at[k, r, core]
        return remote(block, block, x_send.at[r, k], x_recv.at[r, k], other_core)

    def x_wait(k):
        for r in range(2):
            block = keys.at[k, r, other]
            remote(block, block, x_send.at[r, k], x_recv.at[r, k], other_core).wait_recv()

    for k in (1, 3):
        for r in range(2):
            two_copy(r, k).start()
    for r in range(2):
        x_copy(r, 0).start()

    def key_places(k):
        lane = iota((1, CHUNK), 1)
        piece = lane >> 4
        route = jnp.where(piece >= 24, 1, 0)
        rest = piece - 24 * route
        parity = jnp.where(rest >= 12, 1, 0)
        rest = rest - 12 * parity
        dist = (rest * 11) >> 5
        slot = rest - 3 * dist + 3 * route
        x_src = (x + jnp.where(route == 0, dist, k)) & 3
        y_src = (y + jnp.where(route == 0, k, dist)) & 3
        z_src = (slot - (y_src * 2 + (x_src & 1))) & 7
        ctx_src = z_src * 2 + (x_src >> 1)
        span = jnp.zeros_like(lane)
        for i in range(16):
            span = jnp.where(ctx_src == i, span_map[i], span)
        return span * SPAN + (2 * slot + parity) * PIECE + (lane & 15)

    def attend(k):
        ks = keys.at[k]
        allowed = key_places(k) <= q_limit

        def scores(g):
            return nt(
                q_all[2 * g : 2 * g + 2].reshape(2 * ROWS, WIDTH), ks[...].reshape(CHUNK, WIDTH)
            )

        s = scores(0)
        for g in range(4):
            s_next = scores(g + 1) if g < 3 else None
            hs = slice(2 * g, 2 * g + 2)
            s = jnp.where(allowed, s * SCALE2, MASKED)
            old = best[hs].reshape(2 * ROWS, 1)
            new = jnp.maximum(old, jnp.max(s, axis=1, keepdims=True))
            w = jnp.exp2(s - new)
            factor = jnp.exp2(old - new)
            best[hs] = new.reshape(2, ROWS, 1)
            total[hs] = total[hs] * factor.reshape(2, ROWS, 1) + jnp.sum(
                w, axis=1, keepdims=True
            ).reshape(2, ROWS, 1)
            summed = jnp.dot(
                w.astype(BF16), ks[..., :LAT].reshape(CHUNK, LAT), preferred_element_type=F32
            )
            acc[hs] = acc[hs] * factor.reshape(2, ROWS, 1) + summed.reshape(2, ROWS, LAT)
            s = s_next

    x_wait(0)
    attend(0)
    for k in (1, 3):
        for r in range(2):
            two_copy(r, k).wait_recv()
            fwd_copy(r, k).start()
            x_copy(r, k).start()
    x_wait(1)
    attend(1)
    for r in range(2):
        for k in (1, 3):
            fwd_copy(r, k).wait_recv()
        x_copy(r, 2).start()
    x_wait(3)
    attend(3)
    x_wait(2)
    attend(2)

    loads[4].wait()
    for h in range(HEADS):
        context = (acc[h] / total[h]).astype(BF16)
        value = jnp.dot(context, w_uv[h], preferred_element_type=F32)
        o_f[pl.ds(h, SPAN, stride=HEADS), :] = value[:SPAN]
        do_f[pl.ds(h, STEPS * REQS, stride=HEADS), :] = value[SPAN:]
    out[...] = o_f[...].reshape(SPAN, HEADS, VDIM).astype(BF16)
    dec_out[...] = do_f[...].reshape(STEPS, REQS, HEADS, VDIM).astype(BF16)

    for n, (k, route, parity, spot) in enumerate(cache_spots):
        cache[n * PIECE : (n + 1) * PIECE, :] = keys[k, route, parity, spot]

    for j in range(1, 8):
        slot, copy = rs_copy(j)

        @pl.when(slot != 7)
        def _():
            copy.wait_send()

    @pl.when(own < 6)
    def _():
        for j in range(1, 8):
            z_copy(j).wait_send()

    @pl.when(own == 6)
    def _():
        for j in range(1, 8):
            d_copy(j).wait_send()

    for r in range(2):
        for j in range(1, 4):
            one_copy(r, j).wait_send()
        for k in (1, 3):
            two_copy(r, k).wait_send()
            fwd_copy(r, k).wait_send()
        for k in range(4):
            x_copy(r, k).wait_send()


def shards(
    hidden,
    dec_hidden,
    w_down,
    latent_gain,
    query,
    dec_query,
    w_uk,
    w_uv,
    span_map,
    prompt_len,
    block_slot,
):
    rates = (10000.0 ** (-np.arange(ROPE // 2, dtype=np.float32) / np.float32(ROPE // 2))).astype(
        np.float32
    )
    rates = jnp.asarray(np.concatenate([rates, rates])[None, :])
    hbm = pl.BlockSpec(memory_space=pl.ANY)
    vmem = pl.BlockSpec(memory_space=pltpu.VMEM)
    smem = pl.BlockSpec(memory_space=pltpu.SMEM)
    dma = pltpu.SemaphoreType.DMA
    return pl.pallas_call(
        kernel,
        out_shape=(
            pltpu.VMEM((SPAN, HEADS, VDIM), BF16),
            pltpu.VMEM((STEPS, REQS, HEADS, VDIM), BF16),
            pltpu.VMEM((384, WIDTH), BF16),
        ),
        in_specs=[hbm, vmem, hbm, vmem, hbm, vmem, hbm, hbm, vmem, smem, smem, smem],
        out_specs=(vmem, vmem, vmem),
        scratch_shapes=[
            pltpu.VMEM((SPAN, 320), BF16),
            pltpu.VMEM((320, WIDTH), BF16),
            pltpu.VMEM((SPAN, HEADS, NOPE + ROPE), BF16),
            pltpu.VMEM((HEADS, NOPE, LAT), BF16),
            pltpu.VMEM((HEADS, LAT, VDIM), BF16),
            pltpu.VMEM((STEPS * REQS, 320), F32),
            pltpu.VMEM((2, 7, PIECE, WIDTH), F32),
            pltpu.VMEM((7, PIECE, WIDTH), F32),
            pltpu.VMEM((7, PIECE, WIDTH), F32),
            pltpu.VMEM((8, PIECE, WIDTH), F32),
            pltpu.VMEM((4, 2, 2, 12, PIECE, WIDTH), BF16),
            pltpu.VMEM((PIECE, WIDTH), BF16),
            pltpu.VMEM((2, SPAN * HEADS, NOPE), F32),
            pltpu.VMEM((2, STEPS * REQS * HEADS, NOPE), F32),
            pltpu.VMEM((HEADS, ROWS, WIDTH), BF16),
            pltpu.VMEM((HEADS, ROWS, LAT), F32),
            pltpu.VMEM((HEADS, ROWS, 1), F32),
            pltpu.VMEM((HEADS, ROWS, 1), F32),
            pltpu.VMEM((SPAN * HEADS, VDIM), F32),
            pltpu.VMEM((STEPS * REQS * HEADS, VDIM), F32),
            dma((5,)),
            dma((2,)),
            dma((8,)),
            dma((8,)),
            dma((8,)),
            dma((8,)),
            dma((1,)),
            dma((2, 4)),
            dma((2, 4)),
            dma((2, 4)),
            dma((2, 4)),
            dma((2, 4)),
            dma((2, 4)),
            dma((2, 4)),
            dma((2, 4)),
        ],
        compiler_params=pltpu.CompilerParams(
            collective_id=0, has_side_effects=True, vmem_limit_bytes=56 * 2**20
        ),
    )(
        hidden,
        dec_hidden,
        w_down,
        latent_gain.reshape(1, LAT),
        query,
        dec_query,
        w_uk,
        w_uv,
        rates,
        span_map,
        prompt_len,
        block_slot,
    )


def solution(mesh):
    in_specs = (
        P("ctx", ("dec", "grp")),
        P(None, "ctx", ("dec", "grp")),
        P(("dec", "grp"), None),
        P(),
        P("ctx", ("dec", "grp"), None),
        P(None, "ctx", ("dec", "grp"), None),
        P(("dec", "grp"), None, None),
        P(("dec", "grp"), None, None),
        P(),
        P("ctx"),
        P(),
    )
    out_specs = (
        P("ctx", ("dec", "grp"), None),
        P(None, "ctx", ("dec", "grp"), None),
        P("dec", None),
    )
    return jax.shard_map(shards, mesh=mesh, in_specs=in_specs, out_specs=out_specs, check_vma=False)
```

```python
import math

import jax
import jax.numpy as jnp
import numpy as np
from jax import lax
from jax.experimental import pallas as pl
from jax.experimental.pallas import tpu as pltpu
from jax.sharding import PartitionSpec as P

F32 = jnp.float32
BF16 = jnp.bfloat16
MESH = pl.DeviceIdType.MESH

EPSILON = 1e-06
SPAN = 192
HEADS = 8
STEPS = 4
REQS = 4
NOPE = 128
ROPE = 64
LAT = 512
WIDTH = LAT + ROPE
VDIM = 128
PIECE = 16
ROWS = SPAN + STEPS * REQS
CHUNK = 768
BLK = 64
SCALE2 = (NOPE + ROPE) ** -0.5 * math.log2(math.e)
Z_ORDER = (4, 3, 5, 2, 6, 1, 7)
D_ORDER = (5, 3, 4, 6, 2, 7, 1)
MASKED = -2e30
LOWEST = -1e30


def iota(shape, dim):
    return lax.broadcasted_iota(jnp.int32, shape, dim)


def nt(a, b):
    return lax.dot_general(a, b, (((1,), (1,)), ((), ())), preferred_element_type=F32)


def swapped(v):
    half = v.shape[-1] // 2
    return jnp.concatenate([v[:, half:], v[:, :half]], axis=1)


def tables(places, rates):
    angle = places.astype(F32) * rates
    sign = jnp.where(iota((1, ROPE), 1) < ROPE // 2, -1.0, 1.0)
    return jnp.cos(angle), jnp.sin(angle) * sign


def dec_rows_value(prompt_len, row):
    request = row & (REQS - 1)
    value = jnp.zeros_like(row)
    for b in range(REQS):
        value = jnp.where(request == b, prompt_len[b], value)
    return value


def kernel(
    hidden_h,
    dec_hidden,
    w_down_h,
    gain,
    query_h,
    dec_query,
    w_uk_h,
    w_uv_h,
    rates,
    span_map,
    prompt_len,
    block_slot,
    out,
    dec_out,
    cache,
    hidden,
    w_down,
    query,
    w_uk,
    w_uv,
    dec_f,
    part,
    from_core,
    sums,
    arrived,
    keys,
    dec_lat,
    q_f,
    dq_f,
    q_all,
    acc,
    best,
    total,
    o_f,
    do_f,
    load_sem,
    core_sem,
    rs_send,
    rs_recv,
    z_send,
    z_recv,
    d_recv,
    one_send,
    one_recv,
    two_send,
    two_recv,
    fwd_send,
    fwd_recv,
    x_send,
    x_recv,
):
    ctx = lax.axis_index("ctx")
    dec = lax.axis_index("dec")
    core = lax.axis_index("grp")
    z, x_hi = ctx // 2, ctx % 2
    y, x_lo = dec // 2, dec % 2
    x = x_hi * 2 + x_lo
    other = 1 - core

    def at(x_, y_, z_, c_):
        return (z_ * 2 + x_ // 2, y_ * 2 + x_ % 2, c_)

    def remote(src, dst, send, recv, device):
        return pltpu.make_async_remote_copy(
            src_ref=src,
            dst_ref=dst,
            send_sem=send,
            recv_sem=recv,
            device_id=device,
            device_id_type=MESH,
        )

    me = (ctx, dec, core)
    other_core = (ctx, dec, other)
    x_step = lambda j: at((x + j) % 4, y, z, core)
    y_step = lambda j: at(x, (y + j) % 4, z, core)
    z_step = lambda j: (((z + j) % 8) * 2 + x_hi, dec, core)
    d_step = lambda j: (ctx, (dec + j) % 8, core)
    along = (x_step, y_step)

    loads = [
        pltpu.make_async_copy(src, dst, load_sem.at[i])
        for i, (src, dst) in enumerate(
            ((hidden_h, hidden), (w_down_h, w_down), (query_h, query), (w_uk_h, w_uk), (w_uv_h, w_uv))
        )
    ]
    for load in loads:
        load.start()

    barrier = pltpu.get_barrier_semaphore()
    greeted = [z_step(j) for j in Z_ORDER]
    greeted += [d_step(j) for j in D_ORDER]
    greeted += [(z * 2 + 1 - x_hi, y * 2 + lo, core) for lo in range(2)]
    greeted += [other_core]
    for device in greeted:
        pl.semaphore_signal(barrier, inc=1, device_id=device, device_id_type=MESH)

    for t in range(STEPS):
        dec_f[t * REQS : (t + 1) * REQS, :] = dec_hidden[t].astype(F32)
    loads[0].wait()
    loads[1].wait()
    weights = w_down[...]
    partial = jnp.dot(hidden[...], weights, preferred_element_type=F32)
    for piece in range(12):
        part[piece % 2, piece // 2] = partial[piece * PIECE : (piece + 1) * PIECE]
    partial = jnp.dot(dec_f[...].astype(BF16), weights, preferred_element_type=F32)
    part[0, 6] = partial
    part[1, 6] = partial

    blocks = [jnp.int32(0)] * 6
    cache_spots = []
    for b in range(48):
        slot = block_slot[b]
        for i in range(6):
            blocks[i] = jnp.where(slot == dec * 6 + i, b, blocks[i])
    for i in range(6):
        span = blocks[i] // 3
        c_src = jnp.int32(0)
        for c in range(16):
            c_src = jnp.where(span_map[c] == span, c, c_src)
        z_from, hi_from = c_src >> 1, c_src & 1
        for n in range(4):
            piece = (blocks[i] - span * 3) * 4 + n
            parity, slot = piece & 1, piece >> 1
            d_from = (slot - z_from) & 7
            dy = ((d_from >> 1) - y) & 3
            dx = (hi_from * 2 + (d_from & 1) - x) & 3
            first = slot < 3
            k = jnp.where(first, dy, dx)
            spot = jnp.where(first, dx, dy) * 3 + slot - jnp.where(first, 0, 3)
            cache_spots.append((k, jnp.where(first, 0, 1), parity, spot))

    pl.semaphore_wait(barrier, len(greeted))

    swap = remote(part.at[other], from_core, core_sem.at[0], core_sem.at[1], other_core)
    swap.start()

    row = iota((ROWS, 1), 0)
    my_start = span_map[ctx] * SPAN
    lengths = dec_rows_value(prompt_len, row)
    is_dec = row >= SPAN
    places = jnp.where(is_dec, lengths + ((row - SPAN) >> 2), my_start + row)
    q_limit = jnp.where(is_dec, lengths - 1, my_start + row)
    cosine, sine = tables(places, rates[...])
    q_limit = jnp.concatenate([q_limit, q_limit], axis=0)

    loads[2].wait()
    loads[3].wait()
    wide = query[...].astype(F32).reshape(SPAN * HEADS, NOPE + ROPE)
    q_f[0] = wide[:, :NOPE]
    q_f[1, :, :ROPE] = wide[:, NOPE:]
    wide = dec_query[...].astype(F32).reshape(STEPS * REQS * HEADS, NOPE + ROPE)
    dq_f[0] = wide[:, :NOPE]
    dq_f[1, :, :ROPE] = wide[:, NOPE:]

    def absorb(h):
        def both(i):
            mine = q_f[i, pl.ds(h, SPAN, stride=HEADS), :]
            decs = dq_f[i, pl.ds(h, STEPS * REQS, stride=HEADS), :]
            return jnp.concatenate([mine, decs], axis=0)

        nope = both(0).astype(BF16)
        q_all[h, :, :LAT] = jnp.dot(nope, w_uk[h], preferred_element_type=F32).astype(BF16)
        rope = both(1)[:, :ROPE]
        q_all[h, :, LAT:] = (rope * cosine + swapped(rope) * sine).astype(BF16)

    for h in range(4):
        absorb(h)

    swap.wait()
    for s in range(7):
        sums[s] = part[core, s] + from_core[s]

    def rs_copy(j):
        slot = (dec + j + z) % 8
        return slot, remote(
            sums.at[jnp.minimum(slot, 6)], arrived.at[j], rs_send.at[j], rs_recv.at[j], d_step(j)
        )

    for j in D_ORDER:
        slot, copy = rs_copy(j)

        @pl.when(slot != 7)
        def _():
            copy.start()

    for h in range(4, HEADS):
        absorb(h)

    own = (dec + z) % 8
    safe = jnp.minimum(own, 5)
    home = keys.at[0, safe // 3, core, safe % 3]

    @pl.when(own != 7)
    def _():
        raw = sums[jnp.minimum(own, 6)]
        for j in range(1, 8):
            rs_copy(j)[1].wait_recv()
            raw = raw + arrived[j]
        i = iota((PIECE, 1), 0)
        prompt_places = my_start + (2 * own + core) * PIECE + i
        dec_places = dec_rows_value(prompt_len, i) + (i >> 2)
        spots = jnp.where(own == 6, dec_places, prompt_places)
        cos_k, sin_k = tables(spots, rates[...])
        lat = raw[:, :LAT]
        square = jnp.mean(lat * lat, axis=1, keepdims=True)
        lat = lat * lax.rsqrt(square + EPSILON) * gain[...]
        rope = raw[:, LAT:]
        rope = rope * cos_k + swapped(rope) * sin_k
        done = jnp.concatenate([lat, rope], axis=1).astype(BF16)

        @pl.when(own < 6)
        def _():
            keys[0, safe // 3, core, safe % 3] = done

        @pl.when(own == 6)
        def _():
            dec_lat[...] = done

    def z_copy(j):
        return remote(home, home, z_send.at[j], z_recv.at[safe], z_step(j))

    def d_copy(j):
        return remote(dec_lat, dec_lat, z_send.at[j], d_recv.at[0], d_step(j))

    @pl.when(own < 6)
    def _():
        for j in Z_ORDER:
            z_copy(j).start()

    @pl.when(own == 6)
    def _():
        for j in D_ORDER:
            d_copy(j).start()

    for s in range(6):

        @pl.when(own != s)
        def _():
            spot = keys.at[0, s // 3, core, s % 3]
            remote(spot, spot, z_send.at[0], z_recv.at[s], me).wait_recv()

    def one_copy(r, j):
        return remote(
            keys.at[0, r, core, pl.ds(0, 3)],
            keys.at[0, r, core, pl.ds(3 * (4 - j), 3)],
            one_send.at[r, j],
            one_recv.at[r, 4 - j],
            along[r](j),
        )

    for j in (2, 1, 3):
        for r in range(2):
            one_copy(r, j).start()

    @pl.when(own != 6)
    def _():
        d_copy(1).wait_recv()

    best[...] = jnp.full(best.shape, LOWEST, F32)
    total[...] = jnp.zeros(total.shape, F32)
    acc[...] = jnp.zeros(acc.shape, F32)
    fresh_keys = dec_lat[...]
    count = HEADS * STEPS * REQS
    fresh = nt(q_all[:, SPAN:, :].reshape(count, WIDTH), fresh_keys) * SCALE2
    r_, c_ = iota((count, PIECE), 0), iota((count, PIECE), 1)
    fresh_ok = jnp.logical_and((r_ & 3) == (c_ & 3), (c_ >> 2) <= ((r_ & 15) >> 2))
    fresh = jnp.where(fresh_ok, fresh, MASKED)
    top = jnp.max(fresh, axis=1, keepdims=True)
    weight = jnp.exp2(fresh - top)
    best[:, SPAN:, :] = top.reshape(HEADS, 16, 1)
    total[:, SPAN:, :] = jnp.sum(weight, axis=1, keepdims=True).reshape(HEADS, 16, 1)
    acc[:, SPAN:, :] = jnp.dot(
        weight.astype(BF16), fresh_keys[:, :LAT], preferred_element_type=F32
    ).reshape(HEADS, 16, LAT)

    for j in (1, 3, 2):
        for r in range(2):
            one_copy(r, j).wait_recv()

    def two_copy(r, k):
        return remote(
            keys.at[0, r, core], keys.at[k, r, core], two_send.at[r, k], two_recv.at[r, k], along[1 - r](4 - k)
        )

    def fwd_copy(r, k):
        half = pl.ds(0, 6) if k == 1 else pl.ds(6, 6)
        return remote(
            keys.at[k, r, core, half],
            keys.at[2, r, core, half],
            fwd_send.at[r, k],
            fwd_recv.at[r, k],
            along[1 - r](4 - k),
        )

    def x_copy(r, k):
        block = keys.at[k, r, core]
        return remote(block, block, x_send.at[r, k], x_recv.at[r, k], other_core)

    def x_wait(k):
        for r in range(2):
            block = keys.at[k, r, other]
            remote(block, block, x_send.at[r, k], x_recv.at[r, k], other_core).wait_recv()

    for k in (1, 3):
        for r in range(2):
            two_copy(r, k).start()
    for r in range(2):
        x_copy(r, 0).start()

    def key_places(k):
        lane = iota((1, CHUNK), 1)
        piece = lane >> 4
        route = jnp.where(piece >= 24, 1, 0)
        rest = piece - 24 * route
        parity = jnp.where(rest >= 12, 1, 0)
        rest = rest - 12 * parity
        dist = (rest * 11) >> 5
        slot = rest - 3 * dist + 3 * route
        x_src = (x + jnp.where(route == 0, dist, k)) & 3
        y_src = (y + jnp.where(route == 0, k, dist)) & 3
        z_src = (slot - (y_src * 2 + (x_src & 1))) & 7
        ctx_src = z_src * 2 + (x_src >> 1)
        span = jnp.zeros_like(lane)
        for i in range(16):
            span = jnp.where(ctx_src == i, span_map[i], span)
        return span * SPAN + (2 * slot + parity) * PIECE + (lane & 15)

    def attend(k):
        ks = keys.at[k]
        allowed = key_places(k) <= q_limit

        def scores(g):
            return nt(
                q_all[2 * g : 2 * g + 2].reshape(2 * ROWS, WIDTH), ks[...].reshape(CHUNK, WIDTH)
            )

        s = scores(0)
        for g in range(4):
            s_next = scores(g + 1) if g < 3 else None
            hs = slice(2 * g, 2 * g + 2)
            s = jnp.where(allowed, s * SCALE2, MASKED)
            old = best[hs].reshape(2 * ROWS, 1)
            new = jnp.maximum(old, jnp.max(s, axis=1, keepdims=True))
            w = jnp.exp2(s - new)
            factor = jnp.exp2(old - new)
            best[hs] = new.reshape(2, ROWS, 1)
            total[hs] = total[hs] * factor.reshape(2, ROWS, 1) + jnp.sum(
                w, axis=1, keepdims=True
            ).reshape(2, ROWS, 1)
            summed = jnp.dot(
                w.astype(BF16), ks[..., :LAT].reshape(CHUNK, LAT), preferred_element_type=F32
            )
            acc[hs] = acc[hs] * factor.reshape(2, ROWS, 1) + summed.reshape(2, ROWS, LAT)
            s = s_next

    x_wait(0)
    attend(0)
    for k in (1, 3):
        for r in range(2):
            two_copy(r, k).wait_recv()
            fwd_copy(r, k).start()
            x_copy(r, k).start()
    x_wait(1)
    attend(1)
    for r in range(2):
        for k in (1, 3):
            fwd_copy(r, k).wait_recv()
        x_copy(r, 2).start()
    x_wait(3)
    attend(3)
    x_wait(2)
    attend(2)

    loads[4].wait()
    for h in range(HEADS):
        context = (acc[h] / total[h]).astype(BF16)
        value = jnp.dot(context, w_uv[h], preferred_element_type=F32)
        o_f[pl.ds(h, SPAN, stride=HEADS), :] = value[:SPAN]
        do_f[pl.ds(h, STEPS * REQS, stride=HEADS), :] = value[SPAN:]
    out[...] = o_f[...].reshape(SPAN, HEADS, VDIM).astype(BF16)
    dec_out[...] = do_f[...].reshape(STEPS, REQS, HEADS, VDIM).astype(BF16)

    for n, (k, route, parity, spot) in enumerate(cache_spots):
        cache[n * PIECE : (n + 1) * PIECE, :] = keys[k, route, parity, spot]

    for j in range(1, 8):
        slot, copy = rs_copy(j)

        @pl.when(slot != 7)
        def _():
            copy.wait_send()

    @pl.when(own < 6)
    def _():
        for j in range(1, 8):
            z_copy(j).wait_send()

    @pl.when(own == 6)
    def _():
        for j in range(1, 8):
            d_copy(j).wait_send()

    for r in range(2):
        for j in range(1, 4):
            one_copy(r, j).wait_send()
        for k in (1, 3):
            two_copy(r, k).wait_send()
            fwd_copy(r, k).wait_send()
        for k in range(4):
            x_copy(r, k).wait_send()


def shards(
    hidden,
    dec_hidden,
    w_down,
    latent_gain,
    query,
    dec_query,
    w_uk,
    w_uv,
    span_map,
    prompt_len,
    block_slot,
):
    rates = (10000.0 ** (-np.arange(ROPE // 2, dtype=np.float32) / np.float32(ROPE // 2))).astype(
        np.float32
    )
    rates = jnp.asarray(np.concatenate([rates, rates])[None, :])
    hbm = pl.BlockSpec(memory_space=pl.ANY)
    vmem = pl.BlockSpec(memory_space=pltpu.VMEM)
    smem = pl.BlockSpec(memory_space=pltpu.SMEM)
    dma = pltpu.SemaphoreType.DMA
    return pl.pallas_call(
        kernel,
        out_shape=(
            pltpu.VMEM((SPAN, HEADS, VDIM), BF16),
            pltpu.VMEM((STEPS, REQS, HEADS, VDIM), BF16),
            pltpu.VMEM((384, WIDTH), BF16),
        ),
        in_specs=[hbm, vmem, hbm, vmem, hbm, vmem, hbm, hbm, vmem, smem, smem, smem],
        out_specs=(vmem, vmem, vmem),
        scratch_shapes=[
            pltpu.VMEM((SPAN, 320), BF16),
            pltpu.VMEM((320, WIDTH), BF16),
            pltpu.VMEM((SPAN, HEADS, NOPE + ROPE), BF16),
            pltpu.VMEM((HEADS, NOPE, LAT), BF16),
            pltpu.VMEM((HEADS, LAT, VDIM), BF16),
            pltpu.VMEM((STEPS * REQS, 320), F32),
            pltpu.VMEM((2, 7, PIECE, WIDTH), F32),
            pltpu.VMEM((7, PIECE, WIDTH), F32),
            pltpu.VMEM((7, PIECE, WIDTH), F32),
            pltpu.VMEM((8, PIECE, WIDTH), F32),
            pltpu.VMEM((4, 2, 2, 12, PIECE, WIDTH), BF16),
            pltpu.VMEM((PIECE, WIDTH), BF16),
            pltpu.VMEM((2, SPAN * HEADS, NOPE), F32),
            pltpu.VMEM((2, STEPS * REQS * HEADS, NOPE), F32),
            pltpu.VMEM((HEADS, ROWS, WIDTH), BF16),
            pltpu.VMEM((HEADS, ROWS, LAT), F32),
            pltpu.VMEM((HEADS, ROWS, 1), F32),
            pltpu.VMEM((HEADS, ROWS, 1), F32),
            pltpu.VMEM((SPAN * HEADS, VDIM), F32),
            pltpu.VMEM((STEPS * REQS * HEADS, VDIM), F32),
            dma((5,)),
            dma((2,)),
            dma((8,)),
            dma((8,)),
            dma((8,)),
            dma((8,)),
            dma((1,)),
            dma((2, 4)),
            dma((2, 4)),
            dma((2, 4)),
            dma((2, 4)),
            dma((2, 4)),
            dma((2, 4)),
            dma((2, 4)),
            dma((2, 4)),
        ],
        compiler_params=pltpu.CompilerParams(
            collective_id=0, has_side_effects=True, vmem_limit_bytes=56 * 2**20
        ),
    )(
        hidden,
        dec_hidden,
        w_down,
        latent_gain.reshape(1, LAT),
        query,
        dec_query,
        w_uk,
        w_uv,
        rates,
        span_map,
        prompt_len,
        block_slot,
    )


def solution(mesh):
    in_specs = (
        P("ctx", ("dec", "grp")),
        P(None, "ctx", ("dec", "grp")),
        P(("dec", "grp"), None),
        P(),
        P("ctx", ("dec", "grp"), None),
        P(None, "ctx", ("dec", "grp"), None),
        P(("dec", "grp"), None, None),
        P(("dec", "grp"), None, None),
        P(),
        P("ctx"),
        P(),
    )
    out_specs = (
        P("ctx", ("dec", "grp"), None),
        P(None, "ctx", ("dec", "grp"), None),
        P("dec", None),
    )
    return jax.shard_map(shards, mesh=mesh, in_specs=in_specs, out_specs=out_specs, check_vma=False)
```
